32 devices in a mesh: region: 2 (over core), member: 16 (over z, y, x).
Axes of the slice: x: 2, y: 2, z: 4, core: 2. Of those that a mesh axis runs over, the one named last changes fastest.
Arguments:
- state: float32 [512, 16384], P('member', 'region'), may hold values from -6 to 6
- obs_pert: float32 [2, 512, 512], P('region', 'member'), may hold values from -9 to 9
- owners: int32 [2, 512], P('region'), may hold values from 0 to 15, never falling along the last dimension, each value on 1 to 128 neighbouring positions
- loc_index: int32 [2, 512], P('region'), may hold values from 0 to 7
- innov: float32 [2, 512], P('region'), may hold values from -6 to 6
- obs_var: float32 [2, 512], P('region'), may hold values from 0.5 to 2
- loc_scales: float32 [8], replicated, may hold values from 1 to 16
Outputs:
- analysis: float32 [512, 16384], P('member', 'region')
The draws below stay inside these ranges and needn't reach their ends.
Inputs may be any that keep to these rules, and one draw needn't show every extreme that they name: Within each region the owners never fall along the batch, every patch owns at least one observation and some patch owns exactly 4 * 512 // 16.
All inputs are finite; a program needn't handle non-finite values.
Results may differ from the reference program's by a relative error of at most 0.0003.
Values sent between devices are 32-bit elements; how exact they have to be, the bound alone decides.
No kernel may reach another device: no remote copies, remote signals or barrier semaphores. Data moves between devices by JAX's collectives and lax.ppermute only.
A program may use at most 64 MiB of HBM per device.

```python
import math
import jax
import jax.numpy as jnp
import numpy as np
from jax import lax

K = 512
NOBS = 512
NTAB = 8
ITERS = 6
CELLS = 512
NGRID = 8192
N_REGION = 2
N_MEMBER = 16


def draw_obs_pert(key, part):
    key = jax.random.fold_in(key, 11)
    mode_key, noise_key = jax.random.split(key)
    mode_values = jax.random.normal(mode_key, (N_REGION, K, NOBS // 16), jnp.float32)
    common = jnp.repeat(mode_values, 16, axis=2)
    noise_part = jax.random.normal(noise_key, (N_REGION, K, NOBS), jnp.float32)
    values = 1.5 * common + noise_part
    return jnp.clip(values, -9.0, 9.0)


def draw_loc_index(key, part):
    key = jax.random.fold_in(key, 23)
    block_key, switch_key, single_key = jax.random.split(key, 3)
    per_block = jax.random.randint(block_key, (N_REGION, NOBS // 16), 0, NTAB, jnp.int32)
    grouped = jnp.repeat(per_block, 16, axis=1)
    switched = jax.random.randint(switch_key, (N_REGION, NOBS), 0, 8, jnp.int32) == 0
    singles = jax.random.randint(single_key, (N_REGION, NOBS), 0, NTAB, jnp.int32)
    return jnp.where(switched, singles, grouped)


def shard_levels(own_key, extent, pieces, least, top_value):
    def one(dim, blocks):
        draws = jax.random.uniform(jax.random.fold_in(jax.random.fold_in(own_key, 6), dim), (blocks,), jnp.float32, least / len(pieces), top_value / len(pieces))
        return jnp.repeat(jnp.exp(draws), extent[dim] // blocks).reshape((-1,) + (1,) * (len(extent) - dim - 1))

    loudness = one(*pieces[0])
    for cut in pieces[1:]:
        loudness = loudness * one(*cut)
    return loudness


def length_profile(amount, total, reach, slope):
    portions = [(1 << 20) // math.isqrt(standing ** slope) + 1 for standing in range(2, amount + 1)]
    rest, counts = total - reach - (amount - 1), [1] * (amount - 1)
    while rest > 0:
        free = [i for i in range(amount - 1) if counts[i] < reach]
        mass, left = sum([portions[i] for i in free]), rest
        for i in free:
            addition = min(reach - counts[i], max(1, left * portions[i] // mass), rest)
            counts[i] = counts[i] + addition
            rest = rest - addition
    return np.array([reach] + counts)


def uneven(rng, amount, total, reach, slope):
    if amount == 2:
        one = jax.random.randint(rng, (), max(1, total - reach), min(reach, total - 1) + 1)
        return jnp.stack([one, total - one])
    sizes = jnp.asarray(length_profile(amount, total, reach, slope), jnp.int32)
    pairs = (amount - 1) // 2
    donor, sink = sizes[1:1 + 2 * pairs:2], sizes[2:2 + 2 * pairs:2]
    slack = jnp.minimum(donor - 1, reach - sink)
    shifted = jax.random.randint(jax.random.fold_in(rng, 1), (pairs,), 0, 1 << 20) % (slack + 1)
    sizes = sizes.at[1:1 + 2 * pairs:2].set(donor - shifted).at[2:2 + 2 * pairs:2].set(sink + shifted)
    return sizes[jax.random.permutation(jax.random.fold_in(rng, 2), amount)]


def normal_values(own_key, shape, scale, most, cuts=(), held_as=jnp.bfloat16):
    values = jax.random.normal(own_key, shape, jnp.float32) * scale
    if len(cuts) > 0:
        values = shard_levels(own_key, shape, cuts, -0.22, 0.18) * values
    return jnp.clip(values, min=-most, max=most).astype(held_as)


def setup_inputs(seed: int = 0) -> dict:
    key_of = jax.random.split(jax.random.key(seed), 8)
    state = normal_values(key_of[0], (K, N_REGION * NGRID), 1.0, 6.0, ((0, 16), (1, 2)), jnp.float32)
    obs_pert = draw_obs_pert(jax.random.fold_in(key_of[7], 71), 0)
    owners = jax.vmap(lambda own: jnp.searchsorted(jnp.cumsum(uneven(own, N_MEMBER, NOBS, 4 * NOBS // N_MEMBER, 2)), jnp.arange(NOBS), side="right"))(jax.random.split(key_of[2], N_REGION)).reshape((N_REGION, NOBS)).astype(jnp.int32)
    loc_index = draw_loc_index(jax.random.fold_in(key_of[7], 71), 0)
    innov = normal_values(key_of[4], (N_REGION, NOBS), 1.0, 6.0, ((0, 2),), jnp.float32)
    obs_var = jnp.clip(jnp.exp(math.log(2.0) - 1.3862944 * jax.random.uniform(key_of[5], (N_REGION, NOBS), jnp.float32) ** shard_levels(key_of[5], (N_REGION, NOBS), ((0, 2),), -0.2, 0.2)), 0.5, 2.0)
    loc_scales = jnp.clip(jnp.exp(jax.random.uniform(key_of[6], (NTAB,), jnp.float32, math.log(1.0), math.log(16.0))), 1.0, 16.0)
    return dict(state=state, obs_pert=obs_pert, owners=owners, loc_index=loc_index, innov=innov, obs_var=obs_var, loc_scales=loc_scales)


precise = lax.Precision.HIGHEST

def root_iterate(matrix):
    order = matrix.shape[0]
    identity = jnp.eye(order, dtype=jnp.float32)
    frob_norm = jnp.sqrt(jnp.sum(matrix * matrix))
    approx = matrix / frob_norm
    inverse_root = identity
    for sweep in range(ITERS):
        update = 1.5 * identity - 0.5 * jnp.dot(inverse_root, approx, precision=precise)
        approx = jnp.dot(approx, update, precision=precise)
        inverse_root = jnp.dot(update, inverse_root, precision=precise)
    return (inverse_root, frob_norm)

def patch_weights(perturb, positions, scales, innovation, variance, global_patch, cycle_len):
    distance = jnp.abs(global_patch - positions)
    distance = jnp.minimum(distance, cycle_len - distance)
    obs_weight = jnp.exp(-(distance / scales) ** 2) / variance
    order = perturb.shape[0]
    gram = jnp.dot(perturb * obs_weight, perturb.T, precision=precise)
    system = gram + (order - 1.0) * jnp.eye(order, dtype=jnp.float32)
    inverse_root, frob_norm = root_iterate(system)
    forcing = jnp.dot(perturb, obs_weight * innovation, precision=precise)
    inner_step = jnp.dot(inverse_root, forcing, precision=precise)
    mean_shift = jnp.dot(inverse_root, inner_step, precision=precise) / frob_norm
    return jnp.sqrt(order - 1.0) * inverse_root / jnp.sqrt(frob_norm) + mean_shift[:, None]

def update_cells(members, weights):
    center = lax.optimization_barrier(jnp.mean(members, axis=0))
    spread = members - center
    return center + jnp.dot(weights.T, spread, precision=precise)

def reference(state, obs_pert, owners, loc_index, innov, obs_var, loc_scales):
    cycle_len = N_REGION * N_MEMBER
    choose = (loc_index[:, :, None] == jnp.arange(NTAB, dtype=jnp.int32)).astype(jnp.float32)
    scales = lax.optimization_barrier(jnp.sum(choose * loc_scales, axis=2)).reshape(-1)
    positions = (jnp.arange(N_REGION, dtype=jnp.int32)[:, None] * N_MEMBER + owners).astype(jnp.float32).reshape(-1)
    perturb = jnp.transpose(obs_pert, (1, 0, 2)).reshape(K, N_REGION * NOBS)
    innovation = innov.reshape(-1)
    variance = obs_var.reshape(-1)

    def one_patch(global_patch):
        weights = patch_weights(perturb, positions, scales, innovation, variance, global_patch.astype(jnp.float32), float(cycle_len))
        members = lax.dynamic_slice_in_dim(state, (global_patch * CELLS).astype(jnp.int32), CELLS, 1)
        return update_cells(members, weights)
    result = lax.map(one_patch, jnp.arange(cycle_len, dtype=jnp.int32))
    return jnp.transpose(result, (1, 0, 2)).reshape(K, cycle_len * CELLS)
```

```python
import jax
import jax.numpy as jnp
from jax import lax
from jax.experimental import pallas as pl
from jax.experimental.pallas import tpu as pltpu
from jax.sharding import PartitionSpec as P

ITERS = 6
BF16 = jnp.bfloat16
F32 = jnp.float32
NN = (((1,), (0,)), ((), ()))
NT = (((1,), (1,)), ((), ()))


def dot(a, b, dims=NN):
    return lax.dot_general(a, b, dims, preferred_element_type=F32)


def split(x):
    high = x.astype(BF16)
    return high, (x - high.astype(F32)).astype(BF16)


def dot3(a, b, dims=NN):
    return dot(a[0], b[0], dims) + dot(a[0], b[1], dims) + dot(a[1], b[0], dims)


def put(ref, x):
    ref[0], ref[1] = split(x)


def get(ref):
    return ref[0], ref[1]


def eye(order):
    shape = (order, order)
    same = lax.broadcasted_iota(jnp.int32, shape, 0) == lax.broadcasted_iota(jnp.int32, shape, 1)
    return jnp.where(same, 1.0, 0.0).astype(F32)


def row_pair(row):
    width = row.shape[1]
    high, low = split(jnp.broadcast_to(row, (8, width)))
    return jnp.concatenate([high.astype(F32), low.astype(F32)], 0).astype(BF16)


def row_dot(row, b, dims=NN):
    pair = row_pair(row)
    both = dot(pair, b[0], dims) + dot(pair, b[1], dims)
    return both[0:1] + both[8:9]


def solve_kernel(place_ref, own_ref, far_ref, info_ref, w_ref, s_ref, z_ref, q_ref, u_ref):
    order, nobs = own_ref.shape
    blocks = place_ref.shape[0] // 2
    rows = order // blocks
    ratio = info_ref[0:1] / info_ref[1:2]
    root = jnp.exp(-0.5 * ratio * ratio) * lax.rsqrt(info_ref[3:4])
    for r, ref in enumerate((own_ref, far_ref)):
        cols = slice(r * nobs, (r + 1) * nobs)
        for p in range(blocks):
            at = pl.multiple_of(place_ref[r * blocks + p] * rows, rows)
            high, low = split(ref[p * rows : (p + 1) * rows, :] * root[:, cols])
            s_ref[0, pl.ds(at, rows), cols] = high
            s_ref[1, pl.ds(at, rows), cols] = low
    s = get(s_ref)
    forcing = row_dot(root * info_ref[2:3], s, NT)
    system = dot3(s, s, NT) + (order - 1.0) * eye(order)
    inv_norm = lax.rsqrt(jnp.sum(system * system))
    first = system * inv_norm
    put(q_ref, first)
    put(z_ref, 1.5 * eye(order) - 0.5 * first)
    put(q_ref, dot3(get(q_ref), get(z_ref)))

    def sweep(i, carry):
        put(u_ref, 1.5 * eye(order) - 0.5 * dot3(get(z_ref), get(q_ref)))
        next_q = dot3(get(q_ref), get(u_ref))
        next_z = dot3(get(u_ref), get(z_ref))
        put(q_ref, next_q)
        put(z_ref, next_z)
        return carry

    lax.fori_loop(0, ITERS - 2, sweep, 0)
    put(u_ref, 1.5 * eye(order) - 0.5 * dot3(get(z_ref), get(q_ref)))
    z = dot3(get(u_ref), get(z_ref))
    put(z_ref, z)
    shift = row_dot(row_dot(forcing, get(z_ref)), get(z_ref)) * inv_norm
    put(w_ref, (jnp.sqrt(order - 1.0) * jnp.sqrt(inv_norm)) * z + shift)


def solve(place, own, far, info):
    order, nobs = own.shape
    vmem = pl.BlockSpec(memory_space=pltpu.VMEM)
    return pl.pallas_call(
        solve_kernel,
        out_shape=jax.ShapeDtypeStruct((2, order, order), BF16),
        in_specs=[pl.BlockSpec(memory_space=pltpu.SMEM), vmem, vmem, vmem],
        out_specs=vmem,
        scratch_shapes=[pltpu.VMEM((2, order, 2 * nobs), BF16)]
        + [pltpu.VMEM((2, order, order), BF16)] * 3,
        compiler_params=pltpu.CompilerParams(vmem_limit_bytes=40 << 20),
        cost_estimate=pl.CostEstimate(
            flops=18 * 3 * 2 * order**3, bytes_accessed=8 * order * nobs, transcendentals=0
        ),
    )(place, own, far, info)


def update_kernel(w_ref, x_ref, o_ref):
    x = x_ref[...]
    center = jnp.mean(x, axis=0, keepdims=True)
    o_ref[...] = center + dot3(get(w_ref), split(x - center))


def update(weights, members):
    vmem = pl.BlockSpec(memory_space=pltpu.VMEM)
    order, cells = members.shape
    return pl.pallas_call(
        update_kernel,
        out_shape=jax.ShapeDtypeStruct(members.shape, F32),
        in_specs=[vmem, vmem],
        out_specs=vmem,
        compiler_params=pltpu.CompilerParams(vmem_limit_bytes=24 << 20),
        cost_estimate=pl.CostEstimate(
            flops=3 * 2 * order * order * cells, bytes_accessed=12 * order * cells, transcendentals=0
        ),
    )(weights, members)


def swap_by(block, count, first, second):
    route = [(i, i ^ first) for i in range(count)]
    route += [(count + i, count + (i ^ second)) for i in range(count)]
    return lax.ppermute(block, ("region", "member"), route)


def gather_rows(shard, count, region):
    low = 1 << (count.bit_length() - 1) // 2
    if low * low != count or shard.shape[0] % 16:
        whole = lax.all_gather(shard, "member", axis=0, tiled=True)
        blocks = whole.shape[0] // 32
        return whole, jnp.arange(2 * blocks, dtype=jnp.int32) % blocks
    far_steps = [step * low for step in range(low)][::-1][:-1]
    near_steps = list(range(low))[::-1][:-1]
    held = shard
    for one, two in ((far_steps, near_steps), (near_steps, far_steps)):
        held = jnp.concatenate([held] + [swap_by(held, count, a, b) for a, b in zip(one, two)])
    far_off, near_off = jnp.array([0] + far_steps), jnp.array([0] + near_steps)
    far_first = (near_off[:, None] ^ far_off[None, :]).reshape(-1)
    near_first = (far_off[:, None] ^ near_off[None, :]).reshape(-1)
    own = jnp.where(region == 0, far_first, near_first)
    other = jnp.where(region == 0, near_first, far_first)
    place = lax.axis_index("member") ^ jnp.concatenate([own, other])
    return held, place.astype(jnp.int32)


def local(state, obs_pert, owners, loc_index, innov, obs_var, loc_scales):
    region = lax.axis_index("region")
    patch_id = lax.axis_index("member")
    npatch = lax.axis_size("member")
    cycle_len = float(lax.axis_size("region") * npatch)
    table = jnp.arange(loc_scales.shape[0], dtype=jnp.int32)
    choose = (loc_index[0][:, None] == table).astype(F32)
    scales = jnp.sum(choose * loc_scales, axis=1)
    positions = (region * npatch + owners[0]).astype(F32)
    obs_info = jnp.stack([positions, scales, innov[0], obs_var[0]])
    regions = [(0, 1), (1, 0)]
    far_info = lax.ppermute(obs_info, "region", regions)
    own_pert, place = gather_rows(obs_pert[0], npatch, region)
    far_pert = lax.ppermute(own_pert, "region", regions)
    info_all = jnp.concatenate([obs_info, far_info], axis=1)
    distance = jnp.abs((region * npatch + patch_id).astype(F32) - info_all[0])
    distance = jnp.minimum(distance, cycle_len - distance)
    info_all = jnp.concatenate([distance[None], info_all[1:]])
    weights = solve(place, own_pert, far_pert, info_all)
    members = lax.all_to_all(state, "member", split_axis=1, concat_axis=0, tiled=True)
    updated = update(weights, members)
    return lax.all_to_all(updated, "member", split_axis=0, concat_axis=1, tiled=True)


def solution(mesh):
    placed = (
        P("member", "region"),
        P("region", "member", None),
        P("region", None),
        P("region", None),
        P("region", None),
        P("region", None),
        P(),
    )
    return jax.shard_map(
        local, mesh=mesh, in_specs=placed, out_specs=P("member", "region"), check_vma=False
    )
```

```python
import functools

import jax
import jax.numpy as jnp
from jax import lax
from jax.experimental import pallas as pl
from jax.experimental.pallas import tpu as pltpu
from jax.sharding import PartitionSpec as P

ITERS = 6
BF16 = jnp.bfloat16
F32 = jnp.float32
NN = (((1,), (0,)), ((), ()))
NT = (((1,), (1,)), ((), ()))


def dot(a, b, dims=NN):
    return lax.dot_general(a, b, dims, preferred_element_type=F32)


def split(x):
    high = x.astype(BF16)
    return high, (x - high.astype(F32)).astype(BF16)


def dot3(a, b, dims=NN):
    return dot(a[0], b[0], dims) + dot(a[0], b[1], dims) + dot(a[1], b[0], dims)


def put(ref, x):
    ref[0], ref[1] = split(x)


def get(ref):
    return ref[0], ref[1]


def eye(order):
    shape = (order, order)
    same = lax.broadcasted_iota(jnp.int32, shape, 0) == lax.broadcasted_iota(jnp.int32, shape, 1)
    return jnp.where(same, 1.0, 0.0).astype(F32)


def row_pair(row):
    width = row.shape[1]
    high, low = split(jnp.broadcast_to(row, (8, width)))
    return jnp.concatenate([high.astype(F32), low.astype(F32)], 0).astype(BF16)


def row_dot(row, b, dims=NN):
    pair = row_pair(row)
    both = dot(pair, b[0], dims) + dot(pair, b[1], dims)
    return both[0:1] + both[8:9]


def pack_kernel(owner_ref, index_ref, innov_ref, var_ref, table_ref, o_ref):
    first = lax.axis_index("region") * lax.axis_size("member")
    index = index_ref[...]
    scale = jnp.zeros(index.shape, F32)
    for entry in range(table_ref.shape[0]):
        scale = jnp.where(index == entry, table_ref[entry], scale)
    o_ref[...] = jnp.zeros(o_ref.shape, F32)
    o_ref[0:1] = (owner_ref[...] + first).astype(F32)
    o_ref[1:2] = scale
    o_ref[2:3] = innov_ref[...]
    o_ref[3:4] = var_ref[...]


def pack(owners, loc_index, innov, obs_var, loc_scales):
    vmem = pl.BlockSpec(memory_space=pltpu.VMEM)
    return pl.pallas_call(
        pack_kernel,
        out_shape=jax.ShapeDtypeStruct((8, owners.shape[1]), F32),
        in_specs=[vmem] * 4 + [pl.BlockSpec(memory_space=pltpu.SMEM)],
        out_specs=vmem,
    )(owners, loc_index, innov, obs_var, loc_scales)


def solve_kernel(orders, count, *refs):
    nparts = (count - 2) // 2
    own_refs, far_refs = refs[:nparts], refs[nparts : 2 * nparts]
    own_info, far_info, w_ref, s_ref, z_ref, q_ref, u_ref = refs[2 * nparts :]
    order = w_ref.shape[1]
    nobs = own_info.shape[1]
    blocks = len(orders[0])
    rows = order // blocks
    region, member = lax.axis_index("region"), lax.axis_index("member")
    nmember = lax.axis_size("member")
    patch = (region * nmember + member).astype(F32)
    cycle = float(nmember * lax.axis_size("region"))
    info = jnp.concatenate([own_info[...], far_info[...]], axis=1)
    dist = jnp.abs(patch - info[0:1])
    ratio = jnp.minimum(dist, cycle - dist) / info[1:2]
    root = jnp.exp(-0.5 * ratio * ratio) * lax.rsqrt(info[3:4])
    for r, parts in enumerate((own_refs, far_refs)):
        cols = slice(r * nobs, (r + 1) * nobs)
        per_part = blocks // nparts
        for p in range(blocks):
            offset = jnp.where(region == r, orders[0][p], orders[1][p])
            block = member ^ offset if nparts > 1 else offset
            at = pl.multiple_of(block * rows, rows)
            place = p % per_part * rows
            data = parts[p // per_part][place : place + rows, :]
            high, low = split(data * root[:, cols])
            s_ref[0, pl.ds(at, rows), cols] = high
            s_ref[1, pl.ds(at, rows), cols] = low
    s = get(s_ref)
    forcing = row_dot(root * info[2:3], s, NT)
    system = dot3(s, s, NT) + (order - 1.0) * eye(order)
    inv_norm = lax.rsqrt(jnp.sum(system * system))
    first = system * inv_norm
    put(q_ref, first)
    put(z_ref, 1.5 * eye(order) - 0.5 * first)
    put(q_ref, dot3(get(q_ref), get(z_ref)))

    def sweep(i, carry):
        put(u_ref, 1.5 * eye(order) - 0.5 * dot3(get(z_ref), get(q_ref)))
        next_q = dot3(get(q_ref), get(u_ref))
        next_z = dot3(get(u_ref), get(z_ref))
        put(q_ref, next_q)
        put(z_ref, next_z)
        return carry

    lax.fori_loop(0, ITERS - 2, sweep, 0)
    put(u_ref, 1.5 * eye(order) - 0.5 * dot3(get(z_ref), get(q_ref)))
    z = dot3(get(u_ref), get(z_ref))
    put(z_ref, z)
    shift = row_dot(row_dot(forcing, get(z_ref)), get(z_ref)) * inv_norm
    put(w_ref, (jnp.sqrt(order - 1.0) * jnp.sqrt(inv_norm)) * z + shift)


def solve(orders, own_parts, far_parts, own_info, far_info):
    order = sum(part.shape[0] for part in own_parts)
    nobs = own_parts[0].shape[1]
    vmem = pl.BlockSpec(memory_space=pltpu.VMEM)
    operands = [*own_parts, *far_parts, own_info, far_info]
    return pl.pallas_call(
        functools.partial(solve_kernel, orders, len(operands)),
        out_shape=jax.ShapeDtypeStruct((2, order, order), BF16),
        in_specs=[vmem] * len(operands),
        out_specs=vmem,
        scratch_shapes=[pltpu.VMEM((2, order, 2 * nobs), BF16)]
        + [pltpu.VMEM((2, order, order), BF16)] * 3,
        compiler_params=pltpu.CompilerParams(vmem_limit_bytes=40 << 20),
        cost_estimate=pl.CostEstimate(
            flops=20 * 3 * 2 * order**3, bytes_accessed=8 * order * nobs, transcendentals=0
        ),
    )(*operands)


def update_kernel(w_ref, x_ref, o_ref):
    x = x_ref[...]
    center = jnp.mean(x, axis=0, keepdims=True)
    o_ref[...] = center + dot3(get(w_ref), split(x - center))


def update(weights, members):
    vmem = pl.BlockSpec(memory_space=pltpu.VMEM)
    order, cells = members.shape
    return pl.pallas_call(
        update_kernel,
        out_shape=jax.ShapeDtypeStruct(members.shape, F32),
        in_specs=[vmem, vmem],
        out_specs=vmem,
        compiler_params=pltpu.CompilerParams(vmem_limit_bytes=24 << 20),
        cost_estimate=pl.CostEstimate(
            flops=3 * 2 * order * order * cells, bytes_accessed=12 * order * cells, transcendentals=0
        ),
    )(weights, members)


def swap_by(block, count, first, second):
    route = [(i, i ^ first) for i in range(count)]
    route += [(count + i, count + (i ^ second)) for i in range(count)]
    return lax.ppermute(block, ("region", "member"), route)


REGIONS = [(0, 1), (1, 0)]


def from_region(block):
    return lax.ppermute(block, "region", REGIONS)


def gather_rows(shard, info, count):
    low = 1 << (count.bit_length() - 1) // 2
    if low * low != count or shard.shape[0] % 16:
        whole = lax.all_gather(shard, "member", axis=0, tiled=True)
        same = list(range(whole.shape[0] // 32))
        return (same, same), [whole], [from_region(whole)], from_region(info)
    far_steps = [step * low for step in range(low)][::-1][:-1]
    near_steps = list(range(low))[::-1][:-1]
    got = [swap_by(shard, count, a, b) for a, b in zip(far_steps, near_steps)]
    held = jnp.concatenate([shard] + got)
    far_info = from_region(info)
    held, far_info = lax.optimization_barrier((held, far_info))
    own = [held] + [swap_by(held, count, a, b) for a, b in zip(near_steps, far_steps)]
    far = [from_region(part) for part in own]
    far_first = [n ^ f for n in [0] + near_steps for f in [0] + far_steps]
    near_first = [f ^ n for f in [0] + far_steps for n in [0] + near_steps]
    return (far_first, near_first), own, far, far_info


def local(state, obs_pert, owners, loc_index, innov, obs_var, loc_scales):
    npatch = lax.axis_size("member")
    info = pack(owners, loc_index, innov, obs_var, loc_scales)
    orders, own, far, far_info = gather_rows(obs_pert[0], info, npatch)
    weights = solve(orders, own, far, info, far_info)
    members = lax.all_to_all(state, "member", split_axis=1, concat_axis=0, tiled=True)
    updated = update(weights, members)
    return lax.all_to_all(updated, "member", split_axis=0, concat_axis=1, tiled=True)


def solution(mesh):
    placed = (
        P("member", "region"),
        P("region", "member", None),
        P("region", None),
        P("region", None),
        P("region", None),
        P("region", None),
        P(),
    )
    return jax.shard_map(
        local, mesh=mesh, in_specs=placed, out_specs=P("member", "region"), check_vma=False
    )
```

```python
import functools

import jax
import jax.numpy as jnp
from jax import lax
from jax.experimental import pallas as pl
from jax.experimental.pallas import tpu as pltpu
from jax.sharding import PartitionSpec as P

ITERS = 6
BF16 = jnp.bfloat16
F32 = jnp.float32
NN = (((1,), (0,)), ((), ()))
NT = (((1,), (1,)), ((), ()))


def dot(a, b, dims=NN):
    return lax.dot_general(a, b, dims, preferred_element_type=F32)


def split(x):
    high = x.astype(BF16)
    return high, (x - high.astype(F32)).astype(BF16)


def dot3(a, b, dims=NN):
    return dot(a[0], b[0], dims) + dot(a[0], b[1], dims) + dot(a[1], b[0], dims)


def put(ref, x):
    ref[0], ref[1] = split(x)


def get(ref):
    return ref[0], ref[1]


def eye(shape):
    same = lax.broadcasted_iota(jnp.int32, shape, 0) == lax.broadcasted_iota(jnp.int32, shape, 1)
    return jnp.where(same, 1.0, 0.0).astype(F32)


def sym_dot(a, b, half, dims=NN, row=None):
    upper = [a[0, :half, :], a[1, :half, :]]
    if row is not None:
        parts = split(jnp.broadcast_to(row, (16, row.shape[1])))
        upper = [jnp.concatenate(pair) for pair in zip(upper, parts)]
    corner = (slice(half, None), slice(None)) if dims is NT else (slice(None), slice(half, None))
    top = dot3(upper, get(b), dims)
    low = dot3(
        (a[0, half:, :], a[1, half:, :]), (b[(0, *corner)], b[(1, *corner)]), dims
    )
    if row is None:
        return top, low
    return top[:half], low, top[half : half + 1]


def put_at(ref, rows, cols, x):
    ref[0, rows, cols], ref[1, rows, cols] = split(x)


def sym_put(ref, top, low, half):
    first, rest = slice(0, half), slice(half, None)
    put_at(ref, first, slice(None), top)
    put_at(ref, rest, rest, low)
    put_at(ref, rest, first, top[:, half:].T)


def pack_kernel(owner_ref, index_ref, innov_ref, var_ref, table_ref, o_ref):
    first = lax.axis_index("region") * lax.axis_size("member")
    index = index_ref[...]
    scale = jnp.zeros(index.shape, F32)
    for entry in range(table_ref.shape[0]):
        scale = jnp.where(index == entry, table_ref[entry], scale)
    o_ref[...] = jnp.zeros(o_ref.shape, F32)
    o_ref[0:1] = (owner_ref[...] + first).astype(F32)
    o_ref[1:2] = scale
    o_ref[2:3] = innov_ref[...]
    o_ref[3:4] = var_ref[...]


def pack(owners, loc_index, innov, obs_var, loc_scales):
    vmem = pl.BlockSpec(memory_space=pltpu.VMEM)
    return pl.pallas_call(
        pack_kernel,
        out_shape=jax.ShapeDtypeStruct((8, owners.shape[1]), F32),
        in_specs=[vmem] * 4 + [pl.BlockSpec(memory_space=pltpu.SMEM)],
        out_specs=vmem,
    )(owners, loc_index, innov, obs_var, loc_scales)


def solve_kernel(orders, count, *refs):
    nparts = (count - 2) // 2
    own_refs, far_refs = refs[:nparts], refs[nparts : 2 * nparts]
    own_info, far_info, w_ref, s_ref, z_ref, q_ref, u_ref = refs[2 * nparts :]
    order = w_ref.shape[1]
    nobs = own_info.shape[1]
    blocks = len(orders[0])
    rows = order // blocks
    region, member = lax.axis_index("region"), lax.axis_index("member")
    nmember = lax.axis_size("member")
    patch = (region * nmember + member).astype(F32)
    cycle = float(nmember * lax.axis_size("region"))
    info = jnp.concatenate([own_info[...], far_info[...]], axis=1)
    dist = jnp.abs(patch - info[0:1])
    ratio = jnp.minimum(dist, cycle - dist) / info[1:2]
    root = jnp.exp(-0.5 * ratio * ratio) * lax.rsqrt(info[3:4])
    for r, parts in enumerate((own_refs, far_refs)):
        cols = slice(r * nobs, (r + 1) * nobs)
        per_part = blocks // nparts
        for p in range(blocks):
            offset = jnp.where(region == r, orders[0][p], orders[1][p])
            block = member ^ offset if nparts > 1 else offset
            at = pl.multiple_of(block * rows, rows)
            place = p % per_part * rows
            data = parts[p // per_part][place : place + rows, :]
            high, low = split(data * root[:, cols])
            s_ref[0, pl.ds(at, rows), cols] = high
            s_ref[1, pl.ds(at, rows), cols] = low
    half = order // 2
    eye_top, eye_low = eye((half, order)), eye((half, half))
    top, low, row = sym_dot(s_ref, s_ref, half, NT, root * info[2:3])
    top, low = top + (order - 1.0) * eye_top, low + (order - 1.0) * eye_low
    corner = top[:, half:]
    inv_norm = lax.rsqrt(jnp.sum(top * top) + jnp.sum(corner * corner) + jnp.sum(low * low))
    top, low = top * inv_norm, low * inv_norm
    sym_put(q_ref, top, low, half)
    sym_put(z_ref, 1.5 * eye_top - 0.5 * top, 1.5 * eye_low - 0.5 * low, half)

    def put_update(top, low):
        shape = top.shape
        sym_put(u_ref, 1.5 * eye(shape) - 0.5 * top, 1.5 * eye(low.shape) - 0.5 * low, half)

    sym_put(q_ref, *sym_dot(q_ref, z_ref, half), half)
    for _ in range(ITERS - 2):
        put_update(*sym_dot(q_ref, z_ref, half))
        next_q = sym_dot(q_ref, u_ref, half)
        next_z = sym_dot(z_ref, u_ref, half)
        sym_put(q_ref, *next_q, half)
        sym_put(z_ref, *next_z, half)
    top, low, row = sym_dot(q_ref, z_ref, half, NN, row)
    put_update(top, low)
    top, low, row = sym_dot(z_ref, u_ref, half, NN, row)
    left = top[:, half:].T
    lanes = 128
    column = jnp.broadcast_to(row, (lanes, order)).T
    upper = jnp.concatenate([column[:half]] * (order // lanes), 1)
    lower = jnp.concatenate([column[half:]] * (half // lanes), 1)
    below = jnp.concatenate(
        [jnp.sum(left * lower, 0, keepdims=True), jnp.sum(low * lower, 0, keepdims=True)], 1
    )
    shift = (jnp.sum(top * upper, 0, keepdims=True) + below) * inv_norm
    gain = jnp.sqrt(order - 1.0) * jnp.sqrt(inv_norm)
    first, rest = slice(0, half), slice(half, None)
    put_at(w_ref, first, slice(None), gain * top + shift)
    put_at(w_ref, rest, rest, gain * low + shift[:, half:])
    put_at(w_ref, rest, first, gain * left + shift[:, :half])


def solve(orders, own_parts, far_parts, own_info, far_info):
    order = sum(part.shape[0] for part in own_parts)
    nobs = own_parts[0].shape[1]
    vmem = pl.BlockSpec(memory_space=pltpu.VMEM)
    operands = [*own_parts, *far_parts, own_info, far_info]
    return pl.pallas_call(
        functools.partial(solve_kernel, orders, len(operands)),
        out_shape=jax.ShapeDtypeStruct((2, order, order), BF16),
        in_specs=[vmem] * len(operands),
        out_specs=vmem,
        scratch_shapes=[pltpu.VMEM((2, order, 2 * nobs), BF16)]
        + [pltpu.VMEM((2, order, order), BF16)] * 3,
        compiler_params=pltpu.CompilerParams(vmem_limit_bytes=40 << 20),
        cost_estimate=pl.CostEstimate(
            flops=20 * 3 * 2 * order**3, bytes_accessed=8 * order * nobs, transcendentals=0
        ),
    )(*operands)


def update_kernel(w_ref, x_ref, o_ref):
    x = x_ref[...]
    center = jnp.mean(x, axis=0, keepdims=True)
    o_ref[...] = center + dot3(get(w_ref), split(x - center))


def update(weights, members):
    vmem = pl.BlockSpec(memory_space=pltpu.VMEM)
    order, cells = members.shape
    return pl.pallas_call(
        update_kernel,
        out_shape=jax.ShapeDtypeStruct(members.shape, F32),
        in_specs=[vmem, vmem],
        out_specs=vmem,
        compiler_params=pltpu.CompilerParams(vmem_limit_bytes=24 << 20),
        cost_estimate=pl.CostEstimate(
            flops=3 * 2 * order * order * cells, bytes_accessed=12 * order * cells, transcendentals=0
        ),
    )(weights, members)


def swap_by(block, count, first, second):
    route = [(i, i ^ first) for i in range(count)]
    route += [(count + i, count + (i ^ second)) for i in range(count)]
    return lax.ppermute(block, ("region", "member"), route)


REGIONS = [(0, 1), (1, 0)]


def from_region(block):
    return lax.ppermute(block, "region", REGIONS)


def gather_rows(shard, info, count):
    low = 1 << (count.bit_length() - 1) // 2
    if low * low != count or shard.shape[0] % 16:
        whole = lax.all_gather(shard, "member", axis=0, tiled=True)
        same = list(range(whole.shape[0] // 32))
        return (same, same), [whole], [from_region(whole)], from_region(info)
    far_steps = [step * low for step in range(low)][::-1][:-1]
    near_steps = list(range(low))[::-1][:-1]
    got = [swap_by(shard, count, a, b) for a, b in zip(far_steps, far_steps)]
    held = jnp.concatenate([shard] + got)
    far_info = from_region(info)
    held, far_info = lax.optimization_barrier((held, far_info))
    own = [held] + [swap_by(held, count, a, b) for a, b in zip(near_steps, near_steps)]
    far = [from_region(part) for part in own]
    far_first = [n ^ f for n in [0] + near_steps for f in [0] + far_steps]
    near_first = [f ^ n for f in [0] + far_steps for n in [0] + near_steps]
    return (far_first, far_first), own, far, far_info


def local(state, obs_pert, owners, loc_index, innov, obs_var, loc_scales):
    npatch = lax.axis_size("member")
    info = pack(owners, loc_index, innov, obs_var, loc_scales)
    orders, own, far, far_info = gather_rows(obs_pert[0], info, npatch)
    weights = solve(orders, own, far, info, far_info)
    members = lax.all_to_all(state, "member", split_axis=1, concat_axis=0, tiled=True)
    updated = update(weights, members)
    return lax.all_to_all(updated, "member", split_axis=0, concat_axis=1, tiled=True)


def solution(mesh):
    placed = (
        P("member", "region"),
        P("region", "member", None),
        P("region", None),
        P("region", None),
        P("region", None),
        P("region", None),
        P(),
    )
    return jax.shard_map(
        local, mesh=mesh, in_specs=placed, out_specs=P("member", "region"), check_vma=False
    )
```

```python
import functools

import jax
import jax.numpy as jnp
from jax import lax
from jax.experimental import pallas as pl
from jax.experimental.pallas import tpu as pltpu
from jax.sharding import PartitionSpec as P

ITERS = 6
BF16 = jnp.bfloat16
F32 = jnp.float32
NN = (((1,), (0,)), ((), ()))
NT = (((1,), (1,)), ((), ()))


def dot(a, b, dims=NN):
    return lax.dot_general(a, b, dims, preferred_element_type=F32)


def split(x):
    high = x.astype(BF16)
    return high, (x - high.astype(F32)).astype(BF16)


def dot3(a, b, dims=NN):
    return dot(a[0], b[0], dims) + dot(a[0], b[1], dims) + dot(a[1], b[0], dims)


def put(ref, x):
    ref[0], ref[1] = split(x)


def get(ref):
    return ref[0], ref[1]


def eye(shape):
    same = lax.broadcasted_iota(jnp.int32, shape, 0) == lax.broadcasted_iota(jnp.int32, shape, 1)
    return jnp.where(same, 1.0, 0.0).astype(F32)


def sym_dot(a, b, half, dims=NN, row=None):
    upper = [a[0, :half, :], a[1, :half, :]]
    if row is not None:
        parts = split(jnp.broadcast_to(row, (16, row.shape[1])))
        upper = [jnp.concatenate(pair) for pair in zip(upper, parts)]
    corner = (slice(half, None), slice(None)) if dims is NT else (slice(None), slice(half, None))
    top = dot3(upper, get(b), dims)
    low = dot3(
        (a[0, half:, :], a[1, half:, :]), (b[(0, *corner)], b[(1, *corner)]), dims
    )
    if row is None:
        return top, low
    return top[:half], low, top[half : half + 1]


def put_at(ref, rows, cols, x):
    ref[0, rows, cols], ref[1, rows, cols] = split(x)


def sym_put(ref, top, low, half):
    first, rest = slice(0, half), slice(half, None)
    put_at(ref, first, slice(None), top)
    put_at(ref, rest, rest, low)
    put_at(ref, rest, first, top[:, half:].T)


def pack_kernel(owner_ref, index_ref, innov_ref, var_ref, table_ref, o_ref):
    first = lax.axis_index("region") * lax.axis_size("member")
    index = index_ref[...]
    scale = jnp.zeros(index.shape, F32)
    for entry in range(table_ref.shape[0]):
        scale = jnp.where(index == entry, table_ref[entry], scale)
    o_ref[...] = jnp.zeros(o_ref.shape, F32)
    o_ref[0:1] = (owner_ref[...] + first).astype(F32)
    o_ref[1:2] = scale
    o_ref[2:3] = innov_ref[...]
    o_ref[3:4] = var_ref[...]


def pack(owners, loc_index, innov, obs_var, loc_scales):
    vmem = pl.BlockSpec(memory_space=pltpu.VMEM)
    return pl.pallas_call(
        pack_kernel,
        out_shape=jax.ShapeDtypeStruct((8, owners.shape[1]), F32),
        in_specs=[vmem] * 4 + [pl.BlockSpec(memory_space=pltpu.SMEM)],
        out_specs=vmem,
    )(owners, loc_index, innov, obs_var, loc_scales)


def region_gram(orders, r, part_refs, info_ref, s_ref):
    order, nobs = s_ref.shape[1:]
    blocks, nparts = len(orders[0]), len(part_refs)
    rows, per_part = order // blocks, blocks // nparts
    region, member = lax.axis_index("region"), lax.axis_index("member")
    nmember = lax.axis_size("member")
    patch = (region * nmember + member).astype(F32)
    cycle = float(nmember * lax.axis_size("region"))
    dist = jnp.abs(patch - info_ref[0:1])
    ratio = jnp.minimum(dist, cycle - dist) / info_ref[1:2]
    root = jnp.exp(-0.5 * ratio * ratio) * lax.rsqrt(info_ref[3:4])
    for p in range(blocks):
        offset = jnp.where(region == r, orders[0][p], orders[1][p])
        block = member ^ offset if nparts > 1 else offset
        at = pl.multiple_of(block * rows, rows)
        place = p % per_part * rows
        high, low = split(part_refs[p // per_part][place : place + rows, :] * root)
        s_ref[0, pl.ds(at, rows), :] = high
        s_ref[1, pl.ds(at, rows), :] = low
    return sym_dot(s_ref, s_ref, order // 2, NT, root * info_ref[2:3])


def gram_kernel(orders, nparts, *refs):
    info_ref, top_ref, low_ref, row_ref, s_ref = refs[nparts:]
    top, low, row = region_gram(orders, 0, refs[:nparts], info_ref, s_ref)
    top_ref[...] = top
    low_ref[...] = low
    row_ref[...] = jnp.broadcast_to(row, row_ref.shape)


def solve_kernel(orders, nparts, *refs):
    info_ref, own_top, own_low, own_row, w_ref, s_ref, z_ref, q_ref, u_ref = refs[nparts:]
    order = w_ref.shape[1]
    top, low, row = region_gram(orders, 1, refs[:nparts], info_ref, s_ref)
    top, low, row = top + own_top[...], low + own_low[...], row + own_row[0:1]
    half = order // 2
    eye_top, eye_low = eye((half, order)), eye((half, half))
    top, low = top + (order - 1.0) * eye_top, low + (order - 1.0) * eye_low
    corner = top[:, half:]
    inv_norm = lax.rsqrt(jnp.sum(top * top) + jnp.sum(corner * corner) + jnp.sum(low * low))
    top, low = top * inv_norm, low * inv_norm
    sym_put(q_ref, top, low, half)
    sym_put(z_ref, 1.5 * eye_top - 0.5 * top, 1.5 * eye_low - 0.5 * low, half)

    def put_update(top, low):
        shape = top.shape
        sym_put(u_ref, 1.5 * eye(shape) - 0.5 * top, 1.5 * eye(low.shape) - 0.5 * low, half)

    sym_put(q_ref, *sym_dot(q_ref, z_ref, half), half)
    for _ in range(ITERS - 2):
        put_update(*sym_dot(q_ref, z_ref, half))
        next_q = sym_dot(q_ref, u_ref, half)
        next_z = sym_dot(z_ref, u_ref, half)
        sym_put(q_ref, *next_q, half)
        sym_put(z_ref, *next_z, half)
    top, low, row = sym_dot(q_ref, z_ref, half, NN, row)
    put_update(top, low)
    top, low, row = sym_dot(z_ref, u_ref, half, NN, row)
    left = top[:, half:].T
    lanes = 128
    column = jnp.broadcast_to(row, (lanes, order)).T
    upper = jnp.concatenate([column[:half]] * (order // lanes), 1)
    lower = jnp.concatenate([column[half:]] * (half // lanes), 1)
    below = jnp.concatenate(
        [jnp.sum(left * lower, 0, keepdims=True), jnp.sum(low * lower, 0, keepdims=True)], 1
    )
    shift = (jnp.sum(top * upper, 0, keepdims=True) + below) * inv_norm
    gain = jnp.sqrt(order - 1.0) * jnp.sqrt(inv_norm)
    first, rest = slice(0, half), slice(half, None)
    put_at(w_ref, first, slice(None), gain * top + shift)
    put_at(w_ref, rest, rest, gain * low + shift[:, half:])
    put_at(w_ref, rest, first, gain * left + shift[:, :half])


def solve(orders, own_parts, far_parts, own_info, far_info):
    order = sum(part.shape[0] for part in own_parts)
    nobs = own_parts[0].shape[1]
    half = order // 2
    vmem = pl.BlockSpec(memory_space=pltpu.VMEM)
    pair = pltpu.VMEM((2, order, order), BF16)
    nparts = len(own_parts)
    shapes = [(half, order), (half, half), (8, order)]
    own = pl.pallas_call(
        functools.partial(gram_kernel, orders, nparts),
        out_shape=[jax.ShapeDtypeStruct(shape, F32) for shape in shapes],
        in_specs=[vmem] * (nparts + 1),
        out_specs=[vmem] * 3,
        scratch_shapes=[pltpu.VMEM((2, order, nobs), BF16)],
        compiler_params=pltpu.CompilerParams(vmem_limit_bytes=24 << 20),
        cost_estimate=pl.CostEstimate(
            flops=3 * 2 * order**3, bytes_accessed=4 * order * nobs, transcendentals=0
        ),
    )(*own_parts, own_info)
    return pl.pallas_call(
        functools.partial(solve_kernel, orders, nparts),
        out_shape=jax.ShapeDtypeStruct((2, order, order), BF16),
        in_specs=[vmem] * (nparts + 4),
        out_specs=vmem,
        scratch_shapes=[pltpu.VMEM((2, order, nobs), BF16), pair, pair, pair],
        compiler_params=pltpu.CompilerParams(vmem_limit_bytes=40 << 20),
        cost_estimate=pl.CostEstimate(
            flops=21 * 3 * 2 * order**3, bytes_accessed=4 * order * nobs, transcendentals=0
        ),
    )(*far_parts, far_info, *own)


def update_kernel(w_ref, x_ref, o_ref):
    x = x_ref[...]
    center = jnp.mean(x, axis=0, keepdims=True)
    o_ref[...] = center + dot3(get(w_ref), split(x - center))


def update(weights, members):
    vmem = pl.BlockSpec(memory_space=pltpu.VMEM)
    order, cells = members.shape
    return pl.pallas_call(
        update_kernel,
        out_shape=jax.ShapeDtypeStruct(members.shape, F32),
        in_specs=[vmem, vmem],
        out_specs=vmem,
        compiler_params=pltpu.CompilerParams(vmem_limit_bytes=24 << 20),
        cost_estimate=pl.CostEstimate(
            flops=3 * 2 * order * order * cells, bytes_accessed=12 * order * cells, transcendentals=0
        ),
    )(weights, members)


def swap_by(block, count, first, second):
    route = [(i, i ^ first) for i in range(count)]
    route += [(count + i, count + (i ^ second)) for i in range(count)]
    return lax.ppermute(block, ("region", "member"), route)


REGIONS = [(0, 1), (1, 0)]


def from_region(block):
    return lax.ppermute(block, "region", REGIONS)


def gather_rows(shard, info, count):
    low = 1 << (count.bit_length() - 1) // 2
    if low * low != count or shard.shape[0] % 16:
        whole = lax.all_gather(shard, "member", axis=0, tiled=True)
        same = list(range(whole.shape[0] // 32))
        return (same, same), [whole], [from_region(whole)], from_region(info)
    far_steps = [step * low for step in range(low)][::-1][:-1]
    near_steps = list(range(low))[::-1][:-1]
    got = [swap_by(shard, count, a, b) for a, b in zip(far_steps, far_steps)]
    held = jnp.concatenate([shard] + got)
    far_info = from_region(info)
    held, far_info = lax.optimization_barrier((held, far_info))
    own = [held] + [swap_by(held, count, a, b) for a, b in zip(near_steps, near_steps)]
    far = [from_region(part) for part in own]
    far_first = [n ^ f for n in [0] + near_steps for f in [0] + far_steps]
    near_first = [f ^ n for f in [0] + far_steps for n in [0] + near_steps]
    return (far_first, far_first), own, far, far_info


def local(state, obs_pert, owners, loc_index, innov, obs_var, loc_scales):
    npatch = lax.axis_size("member")
    info = pack(owners, loc_index, innov, obs_var, loc_scales)
    orders, own, far, far_info = gather_rows(obs_pert[0], info, npatch)
    weights = solve(orders, own, far, info, far_info)
    members = lax.all_to_all(state, "member", split_axis=1, concat_axis=0, tiled=True)
    updated = update(weights, members)
    return lax.all_to_all(updated, "member", split_axis=0, concat_axis=1, tiled=True)


def solution(mesh):
    placed = (
        P("member", "region"),
        P("region", "member", None),
        P("region", None),
        P("region", None),
        P("region", None),
        P("region", None),
        P(),
    )
    return jax.shard_map(
        local, mesh=mesh, in_specs=placed, out_specs=P("member", "region"), check_vma=False
    )
```

```python
import functools

import jax
import jax.numpy as jnp
from jax import lax
from jax.experimental import pallas as pl
from jax.experimental.pallas import tpu as pltpu
from jax.sharding import PartitionSpec as P

ITERS = 6
BF16 = jnp.bfloat16
F32 = jnp.float32
NN = (((1,), (0,)), ((), ()))
NT = (((1,), (1,)), ((), ()))


def dot(a, b, dims=NN):
    return lax.dot_general(a, b, dims, preferred_element_type=F32)


def split(x):
    high = x.astype(BF16)
    return high, (x - high.astype(F32)).astype(BF16)


def dot3(a, b, dims=NN):
    return dot(a[0], b[0], dims) + dot(a[0], b[1], dims) + dot(a[1], b[0], dims)


def put(ref, x):
    ref[0], ref[1] = split(x)


def get(ref):
    return ref[0], ref[1]


def eye(shape):
    same = lax.broadcasted_iota(jnp.int32, shape, 0) == lax.broadcasted_iota(jnp.int32, shape, 1)
    return jnp.where(same, 1.0, 0.0).astype(F32)


def sym_dot(a, b, half, dims=NN, row=None):
    upper = [a[0, :half, :], a[1, :half, :]]
    if row is not None:
        parts = split(jnp.broadcast_to(row, (16, row.shape[1])))
        upper = [jnp.concatenate(pair) for pair in zip(upper, parts)]
    corner = (slice(half, None), slice(None)) if dims is NT else (slice(None), slice(half, None))
    top = dot3(upper, get(b), dims)
    low = dot3(
        (a[0, half:, :], a[1, half:, :]), (b[(0, *corner)], b[(1, *corner)]), dims
    )
    if row is None:
        return top, low
    return top[:half], low, top[half : half + 1]


def put_at(ref, rows, cols, x):
    ref[0, rows, cols], ref[1, rows, cols] = split(x)


def sym_put(ref, top, low, half):
    first, rest = slice(0, half), slice(half, None)
    put_at(ref, first, slice(None), top)
    put_at(ref, rest, rest, low)
    put_at(ref, rest, first, top[:, half:].T)


def pack_kernel(owner_ref, index_ref, innov_ref, var_ref, table_ref, o_ref):
    first = lax.axis_index("region") * lax.axis_size("member")
    index = index_ref[...]
    scale = jnp.zeros(index.shape, F32)
    for entry in range(table_ref.shape[0]):
        scale = jnp.where(index == entry, table_ref[entry], scale)
    o_ref[...] = jnp.zeros(o_ref.shape, F32)
    o_ref[0:1] = (owner_ref[...] + first).astype(F32)
    o_ref[1:2] = scale
    o_ref[2:3] = innov_ref[...]
    o_ref[3:4] = var_ref[...]


def pack(owners, loc_index, innov, obs_var, loc_scales):
    vmem = pl.BlockSpec(memory_space=pltpu.VMEM)
    return pl.pallas_call(
        pack_kernel,
        out_shape=jax.ShapeDtypeStruct((8, owners.shape[1]), F32),
        in_specs=[vmem] * 4 + [pl.BlockSpec(memory_space=pltpu.SMEM)],
        out_specs=vmem,
    )(owners, loc_index, innov, obs_var, loc_scales)


def region_gram(orders, r, part_refs, info_ref, s_ref):
    order, nobs = s_ref.shape[1:]
    blocks, nparts = len(orders[0]), len(part_refs)
    rows, per_part = order // blocks, blocks // nparts
    region, member = lax.axis_index("region"), lax.axis_index("member")
    nmember = lax.axis_size("member")
    patch = (region * nmember + member).astype(F32)
    cycle = float(nmember * lax.axis_size("region"))
    dist = jnp.abs(patch - info_ref[0:1])
    ratio = jnp.minimum(dist, cycle - dist) / info_ref[1:2]
    root = jnp.exp(-0.5 * ratio * ratio) * lax.rsqrt(info_ref[3:4])
    for p in range(blocks):
        offset = jnp.where(region == r, orders[0][p], orders[1][p])
        block = member ^ offset if nparts > 1 else offset
        at = pl.multiple_of(block * rows, rows)
        place = p % per_part * rows
        high, low = split(part_refs[p // per_part][place : place + rows, :] * root)
        s_ref[0, pl.ds(at, rows), :] = high
        s_ref[1, pl.ds(at, rows), :] = low
    return sym_dot(s_ref, s_ref, order // 2, NT, root * info_ref[2:3])


def gram_kernel(orders, nparts, *refs):
    info_ref, top_ref, low_ref, row_ref, s_ref = refs[nparts:]
    top, low, row = region_gram(orders, 0, refs[:nparts], info_ref, s_ref)
    top_ref[...] = top
    low_ref[...] = low
    row_ref[...] = jnp.broadcast_to(row, row_ref.shape)


def solve_kernel(orders, nparts, *refs):
    info_ref, own_top, own_low, own_row, w_ref, s_ref, z_ref, q_ref, u_ref = refs[nparts:]
    order = w_ref.shape[1]
    top, low, row = region_gram(orders, 1, refs[:nparts], info_ref, s_ref)
    top, low, row = top + own_top[...], low + own_low[...], row + own_row[0:1]
    half = order // 2
    eye_top, eye_low = eye((half, order)), eye((half, half))
    top, low = top + (order - 1.0) * eye_top, low + (order - 1.0) * eye_low
    corner = top[:, half:]
    inv_norm = lax.rsqrt(jnp.sum(top * top) + jnp.sum(corner * corner) + jnp.sum(low * low))
    top, low = top * inv_norm, low * inv_norm
    sym_put(q_ref, top, low, half)
    sym_put(z_ref, 1.5 * eye_top - 0.5 * top, 1.5 * eye_low - 0.5 * low, half)

    def put_update(top, low):
        shape = top.shape
        sym_put(u_ref, 1.5 * eye(shape) - 0.5 * top, 1.5 * eye(low.shape) - 0.5 * low, half)

    sym_put(q_ref, *sym_dot(q_ref, z_ref, half), half)
    for _ in range(ITERS - 2):
        put_update(*sym_dot(q_ref, z_ref, half))
        next_q = sym_dot(q_ref, u_ref, half)
        next_z = sym_dot(z_ref, u_ref, half)
        sym_put(q_ref, *next_q, half)
        sym_put(z_ref, *next_z, half)
    top, low, row = sym_dot(q_ref, z_ref, half, NN, row)
    put_update(top, low)
    top, low, row = sym_dot(z_ref, u_ref, half, NN, row)
    left = top[:, half:].T
    lanes = 128
    column = jnp.broadcast_to(row, (lanes, order)).T
    upper = jnp.concatenate([column[:half]] * (order // lanes), 1)
    lower = jnp.concatenate([column[half:]] * (half // lanes), 1)
    below = jnp.concatenate(
        [jnp.sum(left * lower, 0, keepdims=True), jnp.sum(low * lower, 0, keepdims=True)], 1
    )
    shift = (jnp.sum(top * upper, 0, keepdims=True) + below) * inv_norm
    gain = jnp.sqrt(order - 1.0) * jnp.sqrt(inv_norm)
    first, rest = slice(0, half), slice(half, None)
    put_at(w_ref, first, slice(None), gain * top + shift)
    put_at(w_ref, rest, rest, gain * low + shift[:, half:])
    put_at(w_ref, rest, first, gain * left + shift[:, :half])


def solve(orders, own_parts, far_parts, own_info, far_info):
    order = sum(part.shape[0] for part in own_parts)
    nobs = own_parts[0].shape[1]
    half = order // 2
    vmem = pl.BlockSpec(memory_space=pltpu.VMEM)
    pair = pltpu.VMEM((2, order, order), BF16)
    nparts = len(own_parts)
    shapes = [(half, order), (half, half), (8, order)]
    own = pl.pallas_call(
        functools.partial(gram_kernel, orders, nparts),
        out_shape=[jax.ShapeDtypeStruct(shape, F32) for shape in shapes],
        in_specs=[vmem] * (nparts + 1),
        out_specs=[vmem] * 3,
        scratch_shapes=[pltpu.VMEM((2, order, nobs), BF16)],
        compiler_params=pltpu.CompilerParams(vmem_limit_bytes=24 << 20),
        cost_estimate=pl.CostEstimate(
            flops=3 * 2 * order**3, bytes_accessed=4 * order * nobs, transcendentals=0
        ),
    )(*own_parts, own_info)
    return pl.pallas_call(
        functools.partial(solve_kernel, orders, nparts),
        out_shape=jax.ShapeDtypeStruct((2, order, order), BF16),
        in_specs=[vmem] * (nparts + 4),
        out_specs=vmem,
        scratch_shapes=[pltpu.VMEM((2, order, nobs), BF16), pair, pair, pair],
        compiler_params=pltpu.CompilerParams(vmem_limit_bytes=40 << 20),
        cost_estimate=pl.CostEstimate(
            flops=21 * 3 * 2 * order**3, bytes_accessed=4 * order * nobs, transcendentals=0
        ),
    )(*far_parts, far_info, *own)


def update_kernel(w_ref, x_ref, o_ref):
    x = x_ref[...]
    center = jnp.mean(x, axis=0, keepdims=True)
    o_ref[...] = center + dot3(get(w_ref), split(x - center))


def update(weights, members):
    vmem = pl.BlockSpec(memory_space=pltpu.VMEM)
    order, cells = members.shape
    return pl.pallas_call(
        update_kernel,
        out_shape=jax.ShapeDtypeStruct(members.shape, F32),
        in_specs=[vmem, vmem],
        out_specs=vmem,
        compiler_params=pltpu.CompilerParams(vmem_limit_bytes=24 << 20),
        cost_estimate=pl.CostEstimate(
            flops=3 * 2 * order * order * cells, bytes_accessed=12 * order * cells, transcendentals=0
        ),
    )(weights, members)


def swap_by(block, count, first, second):
    route = [(i, i ^ first) for i in range(count)]
    route += [(count + i, count + (i ^ second)) for i in range(count)]
    return lax.ppermute(block, ("region", "member"), route)


REGIONS = [(0, 1), (1, 0)]


def from_region(block):
    return lax.ppermute(block, "region", REGIONS)


def gather_rows(shard, facts, blocks, count):
    low = 1 << (count.bit_length() - 1) // 2
    if low != 4 or low * low != count or shard.shape[0] % 16:
        whole = lax.all_gather(shard, "member", axis=0, tiled=True)
        same = list(range(whole.shape[0] // 32))
        info = pack(*facts)
        return (same, same), [whole], [from_region(whole)], info, from_region(info), blocks
    far_steps = [2 * low, low, 3 * low]
    near_steps = [2, 1, 3]
    got = [swap_by(shard, count, a, b) for a, b in zip(far_steps, far_steps)]
    held = jnp.concatenate([shard] + got)
    held, facts, blocks = lax.optimization_barrier((held, facts, blocks))
    info, blocks = lax.optimization_barrier((pack(*facts), blocks))
    own = [held] + [swap_by(held, count, a, b) for a, b in zip(near_steps, near_steps)]
    far = [from_region(part) for part in own]
    far_first = [n ^ f for n in [0] + near_steps for f in [0] + far_steps]
    near_first = [f ^ n for f in [0] + far_steps for n in [0] + near_steps]
    return (far_first, far_first), own, far, info, from_region(info), blocks


def local(state, obs_pert, owners, loc_index, innov, obs_var, loc_scales):
    npatch = lax.axis_size("member")
    facts = (owners, loc_index, innov, obs_var, loc_scales)
    rows, width = state.shape
    blocks = jnp.swapaxes(state.reshape(rows, npatch, width // npatch), 0, 1)
    orders, own, far, info, far_info, blocks = gather_rows(obs_pert[0], facts, blocks, npatch)
    weights = solve(orders, own, far, info, far_info)
    members = lax.all_to_all(blocks, "member", split_axis=0, concat_axis=0, tiled=True)
    updated = update(weights, members.reshape(rows * npatch, width // npatch))
    return lax.all_to_all(updated, "member", split_axis=0, concat_axis=1, tiled=True)


def solution(mesh):
    placed = (
        P("member", "region"),
        P("region", "member", None),
        P("region", None),
        P("region", None),
        P("region", None),
        P("region", None),
        P(),
    )
    return jax.shard_map(
        local, mesh=mesh, in_specs=placed, out_specs=P("member", "region"), check_vma=False
    )
```

```python
import functools

import jax
import jax.numpy as jnp
from jax import lax
from jax.experimental import pallas as pl
from jax.experimental.pallas import tpu as pltpu
from jax.sharding import PartitionSpec as P

ITERS = 6
BF16 = jnp.bfloat16
F32 = jnp.float32
NN = (((1,), (0,)), ((), ()))
NT = (((1,), (1,)), ((), ()))


def dot(a, b, dims=NN):
    return lax.dot_general(a, b, dims, preferred_element_type=F32)


def split(x):
    high = x.astype(BF16)
    return high, (x - high.astype(F32)).astype(BF16)


def dot3(a, b, dims=NN):
    return dot(a[0], b[0], dims) + dot(a[0], b[1], dims) + dot(a[1], b[0], dims)


def put(ref, x):
    ref[0], ref[1] = split(x)


def get(ref):
    return ref[0], ref[1]


def eye(shape):
    same = lax.broadcasted_iota(jnp.int32, shape, 0) == lax.broadcasted_iota(jnp.int32, shape, 1)
    return jnp.where(same, 1.0, 0.0).astype(F32)


def sym_dot(a, b, half, dims=NN, row=None):
    upper = [a[0, :half, :], a[1, :half, :]]
    if row is not None:
        parts = split(jnp.broadcast_to(row, (16, row.shape[1])))
        upper = [jnp.concatenate(pair) for pair in zip(upper, parts)]
    corner = (slice(half, None), slice(None)) if dims is NT else (slice(None), slice(half, None))
    top = dot3(upper, get(b), dims)
    low = dot3(
        (a[0, half:, :], a[1, half:, :]), (b[(0, *corner)], b[(1, *corner)]), dims
    )
    if row is None:
        return top, low
    return top[:half], low, top[half : half + 1]


def put_at(ref, rows, cols, x):
    ref[0, rows, cols], ref[1, rows, cols] = split(x)


def sym_put(ref, top, low, half):
    first, rest = slice(0, half), slice(half, None)
    put_at(ref, first, slice(None), top)
    put_at(ref, rest, rest, low)
    put_at(ref, rest, first, top[:, half:].T)


def pack_kernel(owner_ref, index_ref, innov_ref, var_ref, table_ref, o_ref):
    first = lax.axis_index("region") * lax.axis_size("member")
    index = index_ref[...]
    scale = jnp.zeros(index.shape, F32)
    for entry in range(table_ref.shape[0]):
        scale = jnp.where(index == entry, table_ref[entry], scale)
    o_ref[...] = jnp.zeros(o_ref.shape, F32)
    o_ref[0:1] = (owner_ref[...] + first).astype(F32)
    o_ref[1:2] = scale
    o_ref[2:3] = innov_ref[...]
    o_ref[3:4] = var_ref[...]


def pack(owners, loc_index, innov, obs_var, loc_scales):
    vmem = pl.BlockSpec(memory_space=pltpu.VMEM)
    return pl.pallas_call(
        pack_kernel,
        out_shape=jax.ShapeDtypeStruct((8, owners.shape[1]), F32),
        in_specs=[vmem] * 4 + [pl.BlockSpec(memory_space=pltpu.SMEM)],
        out_specs=vmem,
    )(owners, loc_index, innov, obs_var, loc_scales)


def region_gram(orders, r, part_refs, info_ref, s_ref):
    order, nobs = s_ref.shape[1:]
    blocks, nparts = len(orders[0]), len(part_refs)
    rows, per_part = order // blocks, blocks // nparts
    region, member = lax.axis_index("region"), lax.axis_index("member")
    nmember = lax.axis_size("member")
    patch = (region * nmember + member).astype(F32)
    cycle = float(nmember * lax.axis_size("region"))
    dist = jnp.abs(patch - info_ref[0:1])
    ratio = jnp.minimum(dist, cycle - dist) / info_ref[1:2]
    root = jnp.exp(-0.5 * ratio * ratio) * lax.rsqrt(info_ref[3:4])
    for p in range(blocks):
        offset = jnp.where(region == r, orders[0][p], orders[1][p])
        block = member ^ offset if nparts > 1 else offset
        at = pl.multiple_of(block * rows, rows)
        place = p % per_part * rows
        high, low = split(part_refs[p // per_part][place : place + rows, :] * root)
        s_ref[0, pl.ds(at, rows), :] = high
        s_ref[1, pl.ds(at, rows), :] = low
    return sym_dot(s_ref, s_ref, order // 2, NT, root * info_ref[2:3])


def gram_kernel(orders, nparts, *refs):
    info_ref, top_ref, low_ref, row_ref, s_ref = refs[nparts:]
    top, low, row = region_gram(orders, 0, refs[:nparts], info_ref, s_ref)
    top_ref[...] = top
    low_ref[...] = low
    row_ref[...] = jnp.broadcast_to(row, row_ref.shape)


def solve_kernel(orders, nparts, *refs):
    info_ref, own_top, own_low, own_row, w_ref, s_ref, z_ref, q_ref, u_ref = refs[nparts:]
    order = w_ref.shape[1]
    top, low, row = region_gram(orders, 1, refs[:nparts], info_ref, s_ref)
    top, low, row = top + own_top[...], low + own_low[...], row + own_row[0:1]
    half = order // 2
    eye_top, eye_low = eye((half, order)), eye((half, half))
    top, low = top + (order - 1.0) * eye_top, low + (order - 1.0) * eye_low
    corner = top[:, half:]
    inv_norm = lax.rsqrt(jnp.sum(top * top) + jnp.sum(corner * corner) + jnp.sum(low * low))
    top, low = top * inv_norm, low * inv_norm
    sym_put(q_ref, top, low, half)
    sym_put(z_ref, 1.5 * eye_top - 0.5 * top, 1.5 * eye_low - 0.5 * low, half)

    def put_update(top, low):
        shape = top.shape
        sym_put(u_ref, 1.5 * eye(shape) - 0.5 * top, 1.5 * eye(low.shape) - 0.5 * low, half)

    sym_put(q_ref, *sym_dot(q_ref, z_ref, half), half)
    for _ in range(ITERS - 2):
        put_update(*sym_dot(q_ref, z_ref, half))
        next_q = sym_dot(q_ref, u_ref, half)
        next_z = sym_dot(z_ref, u_ref, half)
        sym_put(q_ref, *next_q, half)
        sym_put(z_ref, *next_z, half)
    top, low, row = sym_dot(q_ref, z_ref, half, NN, row)
    put_update(top, low)
    top, low, row = sym_dot(z_ref, u_ref, half, NN, row)
    left = top[:, half:].T
    lanes = 128
    column = jnp.broadcast_to(row, (lanes, order)).T
    upper = jnp.concatenate([column[:half]] * (order // lanes), 1)
    lower = jnp.concatenate([column[half:]] * (half // lanes), 1)
    below = jnp.concatenate(
        [jnp.sum(left * lower, 0, keepdims=True), jnp.sum(low * lower, 0, keepdims=True)], 1
    )
    shift = (jnp.sum(top * upper, 0, keepdims=True) + below) * inv_norm
    gain = jnp.sqrt(order - 1.0) * jnp.sqrt(inv_norm)
    first, rest = slice(0, half), slice(half, None)
    put_at(w_ref, first, slice(None), gain * top + shift)
    put_at(w_ref, rest, rest, gain * low + shift[:, half:])
    put_at(w_ref, rest, first, gain * left + shift[:, :half])


def solve(orders, own_parts, far_parts, own_info, far_info):
    order = sum(part.shape[0] for part in own_parts)
    nobs = own_parts[0].shape[1]
    half = order // 2
    vmem = pl.BlockSpec(memory_space=pltpu.VMEM)
    pair = pltpu.VMEM((2, order, order), BF16)
    nparts = len(own_parts)
    shapes = [(half, order), (half, half), (8, order)]
    own = pl.pallas_call(
        functools.partial(gram_kernel, orders, nparts),
        out_shape=[jax.ShapeDtypeStruct(shape, F32) for shape in shapes],
        in_specs=[vmem] * (nparts + 1),
        out_specs=[vmem] * 3,
        scratch_shapes=[pltpu.VMEM((2, order, nobs), BF16)],
        compiler_params=pltpu.CompilerParams(vmem_limit_bytes=24 << 20),
        cost_estimate=pl.CostEstimate(
            flops=3 * 2 * order**3, bytes_accessed=4 * order * nobs, transcendentals=0
        ),
    )(*own_parts, own_info)
    return pl.pallas_call(
        functools.partial(solve_kernel, orders, nparts),
        out_shape=jax.ShapeDtypeStruct((2, order, order), BF16),
        in_specs=[vmem] * (nparts + 4),
        out_specs=vmem,
        scratch_shapes=[pltpu.VMEM((2, order, nobs), BF16), pair, pair, pair],
        compiler_params=pltpu.CompilerParams(vmem_limit_bytes=40 << 20),
        cost_estimate=pl.CostEstimate(
            flops=21 * 3 * 2 * order**3, bytes_accessed=4 * order * nobs, transcendentals=0
        ),
    )(*far_parts, far_info, *own)


def update_kernel(w_ref, x_ref, o_ref):
    x = x_ref[...]
    center = jnp.mean(x, axis=0, keepdims=True)
    o_ref[...] = center + dot3(get(w_ref), split(x - center))


def update(weights, members):
    vmem = pl.BlockSpec(memory_space=pltpu.VMEM)
    order, cells = members.shape
    return pl.pallas_call(
        update_kernel,
        out_shape=jax.ShapeDtypeStruct(members.shape, F32),
        in_specs=[vmem, vmem],
        out_specs=vmem,
        compiler_params=pltpu.CompilerParams(vmem_limit_bytes=24 << 20),
        cost_estimate=pl.CostEstimate(
            flops=3 * 2 * order * order * cells, bytes_accessed=12 * order * cells, transcendentals=0
        ),
    )(weights, members)


def swap_by(block, count, first, second):
    route = [(i, i ^ first) for i in range(count)]
    route += [(count + i, count + (i ^ second)) for i in range(count)]
    return lax.ppermute(block, ("region", "member"), route)


REGIONS = [(0, 1), (1, 0)]


def from_region(block):
    return lax.ppermute(block, "region", REGIONS)


def gather_rows(shard, facts, blocks, count):
    low = 1 << (count.bit_length() - 1) // 2
    if low != 4 or low * low != count or shard.shape[0] % 16:
        whole = lax.all_gather(shard, "member", axis=0, tiled=True)
        same = list(range(whole.shape[0] // 32))
        info = pack(*facts)
        return (same, same), [whole], [from_region(whole)], info, from_region(info), blocks
    far_steps = [(step * low, step * low) for step in (2, 1, 3)]
    near_steps = [(2, 1), (1, 2), (3, 3)]
    got = [swap_by(shard, count, a, b) for a, b in far_steps]
    held = jnp.concatenate([shard] + got)
    held, facts, blocks = lax.optimization_barrier((held, facts, blocks))
    info, blocks = lax.optimization_barrier((pack(*facts), blocks))
    own = [held] + [swap_by(held, count, a, b) for a, b in near_steps]
    far = [from_region(part) for part in own]
    orders = [
        [n ^ f for n in [0] + [pair[r] for pair in near_steps] for f in [0] + [pair[r] for pair in far_steps]]
        for r in (0, 1)
    ]
    return orders, own, far, info, from_region(info), blocks


def local(state, obs_pert, owners, loc_index, innov, obs_var, loc_scales):
    npatch = lax.axis_size("member")
    facts = (owners, loc_index, innov, obs_var, loc_scales)
    rows, width = state.shape
    blocks = jnp.swapaxes(state.reshape(rows, npatch, width // npatch), 0, 1)
    orders, own, far, info, far_info, blocks = gather_rows(obs_pert[0], facts, blocks, npatch)
    weights = solve(orders, own, far, info, far_info)
    members = lax.all_to_all(blocks, "member", split_axis=0, concat_axis=0, tiled=True)
    updated = update(weights, members.reshape(rows * npatch, width // npatch))
    return lax.all_to_all(updated, "member", split_axis=0, concat_axis=1, tiled=True)


def solution(mesh):
    placed = (
        P("member", "region"),
        P("region", "member", None),
        P("region", None),
        P("region", None),
        P("region", None),
        P("region", None),
        P(),
    )
    return jax.shard_map(
        local, mesh=mesh, in_specs=placed, out_specs=P("member", "region"), check_vma=False
    )
```

```python
import functools

import jax
import jax.numpy as jnp
from jax import lax
from jax.experimental import pallas as pl
from jax.experimental.pallas import tpu as pltpu
from jax.sharding import PartitionSpec as P

ITERS = 6
BF16 = jnp.bfloat16
F32 = jnp.float32
NN = (((1,), (0,)), ((), ()))
NT = (((1,), (1,)), ((), ()))


def dot(a, b, dims=NN):
    return lax.dot_general(a, b, dims, preferred_element_type=F32)


def split(x):
    high = x.astype(BF16)
    return high, (x - high.astype(F32)).astype(BF16)


def dot3(a, b, dims=NN):
    return dot(a[0], b[0], dims) + dot(a[0], b[1], dims) + dot(a[1], b[0], dims)


def put(ref, x):
    ref[0], ref[1] = split(x)


def get(ref):
    return ref[0], ref[1]


def eye(shape):
    same = lax.broadcasted_iota(jnp.int32, shape, 0) == lax.broadcasted_iota(jnp.int32, shape, 1)
    return jnp.where(same, 1.0, 0.0).astype(F32)


def sym_dot(a, b, half, dims=NN, row=None):
    upper = [a[0, :half, :], a[1, :half, :]]
    if row is not None:
        parts = split(jnp.broadcast_to(row, (16, row.shape[1])))
        upper = [jnp.concatenate(pair) for pair in zip(upper, parts)]
    corner = (slice(half, None), slice(None)) if dims is NT else (slice(None), slice(half, None))
    top = dot3(upper, get(b), dims)
    low = dot3(
        (a[0, half:, :], a[1, half:, :]), (b[(0, *corner)], b[(1, *corner)]), dims
    )
    if row is None:
        return top, low
    return top[:half], low, top[half : half + 1]


def put_at(ref, rows, cols, x):
    ref[0, rows, cols], ref[1, rows, cols] = split(x)


def sym_put(ref, top, low, half):
    first, rest = slice(0, half), slice(half, None)
    for i, part in enumerate(split(top)):
        ref[i, first, :] = part
        ref[i, rest, first] = part[:, half:].T
    put_at(ref, rest, rest, low)


def pack_kernel(owner_ref, index_ref, innov_ref, var_ref, table_ref, o_ref):
    first = lax.axis_index("region") * lax.axis_size("member")
    index = index_ref[...]
    scale = jnp.zeros(index.shape, F32)
    for entry in range(table_ref.shape[0]):
        scale = jnp.where(index == entry, table_ref[entry], scale)
    o_ref[...] = jnp.zeros(o_ref.shape, F32)
    o_ref[0:1] = (owner_ref[...] + first).astype(F32)
    o_ref[1:2] = scale
    o_ref[2:3] = innov_ref[...]
    o_ref[3:4] = var_ref[...]


def pack(owners, loc_index, innov, obs_var, loc_scales):
    vmem = pl.BlockSpec(memory_space=pltpu.VMEM)
    return pl.pallas_call(
        pack_kernel,
        out_shape=jax.ShapeDtypeStruct((8, owners.shape[1]), F32),
        in_specs=[vmem] * 4 + [pl.BlockSpec(memory_space=pltpu.SMEM)],
        out_specs=vmem,
    )(owners, loc_index, innov, obs_var, loc_scales)


def region_gram(orders, r, part_refs, info_ref, s_ref):
    order, nobs = s_ref.shape[1:]
    blocks, nparts = len(orders[0]), len(part_refs)
    rows, per_part = order // blocks, blocks // nparts
    region, member = lax.axis_index("region"), lax.axis_index("member")
    nmember = lax.axis_size("member")
    patch = (region * nmember + member).astype(F32)
    cycle = float(nmember * lax.axis_size("region"))
    dist = jnp.abs(patch - info_ref[0:1])
    ratio = jnp.minimum(dist, cycle - dist) / info_ref[1:2]
    root = jnp.exp(-0.5 * ratio * ratio) * lax.rsqrt(info_ref[3:4])
    for p in range(blocks):
        offset = jnp.where(region == r, orders[0][p], orders[1][p])
        block = member ^ offset if nparts > 1 else offset
        at = pl.multiple_of(block * rows, rows)
        place = p % per_part * rows
        high, low = split(part_refs[p // per_part][place : place + rows, :] * root)
        s_ref[0, pl.ds(at, rows), :] = high
        s_ref[1, pl.ds(at, rows), :] = low
    return sym_dot(s_ref, s_ref, order // 2, NT, root * info_ref[2:3])


def gram_kernel(orders, nparts, *refs):
    info_ref, top_ref, low_ref, row_ref, s_ref = refs[nparts:]
    top, low, row = region_gram(orders, 0, refs[:nparts], info_ref, s_ref)
    top_ref[...] = top
    low_ref[...] = low
    row_ref[...] = jnp.broadcast_to(row, row_ref.shape)


def solve_kernel(orders, nparts, *refs):
    info_ref, own_top, own_low, own_row, w_ref, s_ref, z_ref, q_ref, u_ref = refs[nparts:]
    order = w_ref.shape[1]
    top, low, row = region_gram(orders, 1, refs[:nparts], info_ref, s_ref)
    top, low, row = top + own_top[...], low + own_low[...], row + own_row[0:1]
    half = order // 2
    eye_top, eye_low = eye((half, order)), eye((half, half))
    top, low = top + (order - 1.0) * eye_top, low + (order - 1.0) * eye_low
    corner = top[:, half:]
    inv_norm = lax.rsqrt(jnp.sum(top * top) + jnp.sum(corner * corner) + jnp.sum(low * low))
    top, low = top * inv_norm, low * inv_norm
    sym_put(q_ref, top, low, half)
    sym_put(z_ref, 1.5 * eye_top - 0.5 * top, 1.5 * eye_low - 0.5 * low, half)

    def put_update(top, low):
        shape = top.shape
        sym_put(u_ref, 1.5 * eye(shape) - 0.5 * top, 1.5 * eye(low.shape) - 0.5 * low, half)

    sym_put(q_ref, *sym_dot(q_ref, z_ref, half), half)
    for _ in range(ITERS - 2):
        put_update(*sym_dot(q_ref, z_ref, half))
        next_q = sym_dot(q_ref, u_ref, half)
        next_z = sym_dot(z_ref, u_ref, half)
        sym_put(q_ref, *next_q, half)
        sym_put(z_ref, *next_z, half)
    top, low, row = sym_dot(q_ref, z_ref, half, NN, row)
    put_update(top, low)
    top, low, row = sym_dot(z_ref, u_ref, half, NN, row)
    left = top[:, half:].T
    lanes = 128
    column = jnp.broadcast_to(row, (lanes, order)).T
    upper = jnp.concatenate([column[:half]] * (order // lanes), 1)
    lower = jnp.concatenate([column[half:]] * (half // lanes), 1)
    below = jnp.concatenate(
        [jnp.sum(left * lower, 0, keepdims=True), jnp.sum(low * lower, 0, keepdims=True)], 1
    )
    shift = (jnp.sum(top * upper, 0, keepdims=True) + below) * inv_norm
    gain = jnp.sqrt(order - 1.0) * jnp.sqrt(inv_norm)
    first, rest = slice(0, half), slice(half, None)
    put_at(w_ref, first, slice(None), gain * top + shift)
    put_at(w_ref, rest, rest, gain * low + shift[:, half:])
    put_at(w_ref, rest, first, gain * left + shift[:, :half])


def solve(orders, own_parts, far_parts, own_info, far_info):
    order = sum(part.shape[0] for part in own_parts)
    nobs = own_parts[0].shape[1]
    half = order // 2
    vmem = pl.BlockSpec(memory_space=pltpu.VMEM)
    pair = pltpu.VMEM((2, order, order), BF16)
    nparts = len(own_parts)
    shapes = [(half, order), (half, half), (8, order)]
    own = pl.pallas_call(
        functools.partial(gram_kernel, orders, nparts),
        out_shape=[jax.ShapeDtypeStruct(shape, F32) for shape in shapes],
        in_specs=[vmem] * (nparts + 1),
        out_specs=[vmem] * 3,
        scratch_shapes=[pltpu.VMEM((2, order, nobs), BF16)],
        compiler_params=pltpu.CompilerParams(vmem_limit_bytes=24 << 20),
        cost_estimate=pl.CostEstimate(
            flops=3 * 2 * order**3, bytes_accessed=4 * order * nobs, transcendentals=0
        ),
    )(*own_parts, own_info)
    return pl.pallas_call(
        functools.partial(solve_kernel, orders, nparts),
        out_shape=jax.ShapeDtypeStruct((2, order, order), BF16),
        in_specs=[vmem] * (nparts + 4),
        out_specs=vmem,
        scratch_shapes=[pltpu.VMEM((2, order, nobs), BF16), pair, pair, pair],
        compiler_params=pltpu.CompilerParams(vmem_limit_bytes=40 << 20),
        cost_estimate=pl.CostEstimate(
            flops=21 * 3 * 2 * order**3, bytes_accessed=4 * order * nobs, transcendentals=0
        ),
    )(*far_parts, far_info, *own)


def update_kernel(w_ref, x_ref, o_ref):
    x = x_ref[...]
    center = jnp.mean(x, axis=0, keepdims=True)
    o_ref[...] = center + dot3(get(w_ref), split(x - center))


def update(weights, members):
    vmem = pl.BlockSpec(memory_space=pltpu.VMEM)
    order, cells = members.shape
    return pl.pallas_call(
        update_kernel,
        out_shape=jax.ShapeDtypeStruct(members.shape, F32),
        in_specs=[vmem, vmem],
        out_specs=vmem,
        compiler_params=pltpu.CompilerParams(vmem_limit_bytes=24 << 20),
        cost_estimate=pl.CostEstimate(
            flops=3 * 2 * order * order * cells, bytes_accessed=12 * order * cells, transcendentals=0
        ),
    )(weights, members)


def swap_by(block, count, first, second):
    route = [(i, i ^ first) for i in range(count)]
    route += [(count + i, count + (i ^ second)) for i in range(count)]
    return lax.ppermute(block, ("region", "member"), route)


REGIONS = [(0, 1), (1, 0)]


def from_region(block):
    return lax.ppermute(block, "region", REGIONS)


def gather_rows(shard, facts, blocks, count):
    low = 1 << (count.bit_length() - 1) // 2
    if low != 4 or low * low != count or shard.shape[0] % 16:
        whole = lax.all_gather(shard, "member", axis=0, tiled=True)
        same = list(range(whole.shape[0] // 32))
        info = pack(*facts)
        return (same, same), [whole], [from_region(whole)], info, from_region(info), blocks
    far_steps = [2 * low, low, 3 * low]
    near_steps = [2, 1, 3]
    got = [swap_by(shard, count, a, b) for a, b in zip(far_steps, far_steps)]
    held = jnp.concatenate([shard] + got)
    held, facts, blocks = lax.optimization_barrier((held, facts, blocks))
    info, blocks = lax.optimization_barrier((pack(*facts), blocks))
    own = [held] + [swap_by(held, count, a, b) for a, b in zip(near_steps, near_steps)]
    far = [from_region(part) for part in own]
    far_first = [n ^ f for n in [0] + near_steps for f in [0] + far_steps]
    near_first = [f ^ n for f in [0] + far_steps for n in [0] + near_steps]
    return (far_first, far_first), own, far, info, from_region(info), blocks


def local(state, obs_pert, owners, loc_index, innov, obs_var, loc_scales):
    npatch = lax.axis_size("member")
    facts = (owners, loc_index, innov, obs_var, loc_scales)
    rows, width = state.shape
    blocks = jnp.swapaxes(state.reshape(rows, npatch, width // npatch), 0, 1)
    orders, own, far, info, far_info, blocks = gather_rows(obs_pert[0], facts, blocks, npatch)
    weights = solve(orders, own, far, info, far_info)
    members = lax.all_to_all(blocks, "member", split_axis=0, concat_axis=0, tiled=True)
    updated = update(weights, members.reshape(rows * npatch, width // npatch))
    return lax.all_to_all(updated, "member", split_axis=0, concat_axis=1, tiled=True)


def solution(mesh):
    placed = (
        P("member", "region"),
        P("region", "member", None),
        P("region", None),
        P("region", None),
        P("region", None),
        P("region", None),
        P(),
    )
    return jax.shard_map(
        local, mesh=mesh, in_specs=placed, out_specs=P("member", "region"), check_vma=False
    )
```

```python
import functools

import jax
import jax.numpy as jnp
from jax import lax
from jax.experimental import pallas as pl
from jax.experimental.pallas import tpu as pltpu
from jax.sharding import PartitionSpec as P

ITERS = 6
BF16 = jnp.bfloat16
F32 = jnp.float32
NN = (((1,), (0,)), ((), ()))
NT = (((1,), (1,)), ((), ()))


def dot(a, b, dims=NN):
    return lax.dot_general(a, b, dims, preferred_element_type=F32)


def split(x):
    high = x.astype(BF16)
    return high, (x - high.astype(F32)).astype(BF16)


def dot3(a, b, dims=NN):
    return dot(a[0], b[0], dims) + dot(a[0], b[1], dims) + dot(a[1], b[0], dims)


def put(ref, x):
    ref[0], ref[1] = split(x)


def get(ref):
    return ref[0], ref[1]


def eye(shape):
    same = lax.broadcasted_iota(jnp.int32, shape, 0) == lax.broadcasted_iota(jnp.int32, shape, 1)
    return jnp.where(same, 1.0, 0.0).astype(F32)


def sym_dot(a, b, half, dims=NN, row=None):
    upper = [a[0, :half, :], a[1, :half, :]]
    if row is not None:
        parts = split(jnp.broadcast_to(row, (16, row.shape[1])))
        upper = [jnp.concatenate(pair) for pair in zip(upper, parts)]
    corner = (slice(half, None), slice(None)) if dims is NT else (slice(None), slice(half, None))
    top = dot3(upper, get(b), dims)
    low = dot3(
        (a[0, half:, :], a[1, half:, :]), (b[(0, *corner)], b[(1, *corner)]), dims
    )
    if row is None:
        return top, low
    return top[:half], low, top[half : half + 1]


def put_at(ref, rows, cols, x):
    ref[0, rows, cols], ref[1, rows, cols] = split(x)


def sym_put(ref, top, low, half):
    first, rest = slice(0, half), slice(half, None)
    for i, part in enumerate(split(top)):
        ref[i, first, :] = part
        ref[i, rest, first] = part[:, half:].T
    put_at(ref, rest, rest, low)


def pack_kernel(owner_ref, index_ref, innov_ref, var_ref, table_ref, o_ref):
    first = lax.axis_index("region") * lax.axis_size("member")
    index = index_ref[...]
    scale = jnp.zeros(index.shape, F32)
    for entry in range(table_ref.shape[0]):
        scale = jnp.where(index == entry, table_ref[entry], scale)
    o_ref[...] = jnp.zeros(o_ref.shape, F32)
    o_ref[0:1] = (owner_ref[...] + first).astype(F32)
    o_ref[1:2] = scale
    o_ref[2:3] = innov_ref[...]
    o_ref[3:4] = var_ref[...]


def pack(owners, loc_index, innov, obs_var, loc_scales):
    vmem = pl.BlockSpec(memory_space=pltpu.VMEM)
    return pl.pallas_call(
        pack_kernel,
        out_shape=jax.ShapeDtypeStruct((8, owners.shape[1]), F32),
        in_specs=[vmem] * 4 + [pl.BlockSpec(memory_space=pltpu.SMEM)],
        out_specs=vmem,
    )(owners, loc_index, innov, obs_var, loc_scales)


def region_gram(orders, r, part_refs, info_ref, s_ref):
    order, nobs = s_ref.shape[1:]
    blocks, nparts = len(orders[0]), len(part_refs)
    rows, per_part = order // blocks, blocks // nparts
    region, member = lax.axis_index("region"), lax.axis_index("member")
    nmember = lax.axis_size("member")
    patch = (region * nmember + member).astype(F32)
    cycle = float(nmember * lax.axis_size("region"))
    dist = jnp.abs(patch - info_ref[0:1])
    ratio = jnp.minimum(dist, cycle - dist) / info_ref[1:2]
    root = jnp.exp(-0.5 * ratio * ratio) * lax.rsqrt(info_ref[3:4])
    for p in range(blocks):
        offset = jnp.where(region == r, orders[0][p], orders[1][p])
        block = member ^ offset if nparts > 1 else offset
        at = pl.multiple_of(block * rows, rows)
        place = p % per_part * rows
        high, low = split(part_refs[p // per_part][place : place + rows, :] * root)
        s_ref[0, pl.ds(at, rows), :] = high
        s_ref[1, pl.ds(at, rows), :] = low
    return sym_dot(s_ref, s_ref, order // 2, NT, root * info_ref[2:3])


def gram_kernel(orders, nparts, *refs):
    info_ref, top_ref, low_ref, row_ref, s_ref = refs[nparts:]
    top, low, row = region_gram(orders, 0, refs[:nparts], info_ref, s_ref)
    top_ref[...] = top
    low_ref[...] = low
    row_ref[...] = jnp.broadcast_to(row, row_ref.shape)


def solve_kernel(orders, nparts, *refs):
    info_ref, own_top, own_low, own_row, w_ref, s_ref, z_ref, q_ref, u_ref = refs[nparts:]
    order = w_ref.shape[1]
    top, low, row = region_gram(orders, 1, refs[:nparts], info_ref, s_ref)
    top, low, row = top + own_top[...], low + own_low[...], row + own_row[0:1]
    half = order // 2
    eye_top, eye_low = eye((half, order)), eye((half, half))
    top, low = top + (order - 1.0) * eye_top, low + (order - 1.0) * eye_low
    corner = top[:, half:]
    inv_norm = lax.rsqrt(jnp.sum(top * top) + jnp.sum(corner * corner) + jnp.sum(low * low))
    top, low = top * inv_norm, low * inv_norm
    sym_put(q_ref, top, low, half)
    sym_put(z_ref, 1.5 * eye_top - 0.5 * top, 1.5 * eye_low - 0.5 * low, half)

    def put_update(top, low):
        shape = top.shape
        sym_put(u_ref, 1.5 * eye(shape) - 0.5 * top, 1.5 * eye(low.shape) - 0.5 * low, half)

    sym_put(q_ref, *sym_dot(q_ref, z_ref, half), half)
    for _ in range(ITERS - 2):
        put_update(*sym_dot(q_ref, z_ref, half))
        next_q = sym_dot(q_ref, u_ref, half)
        next_z = sym_dot(z_ref, u_ref, half)
        sym_put(q_ref, *next_q, half)
        sym_put(z_ref, *next_z, half)
    top, low, row = sym_dot(q_ref, z_ref, half, NN, row)
    put_update(top, low)
    top, low, row = sym_dot(z_ref, u_ref, half, NN, row)
    left = top[:, half:].T
    lanes = 128
    column = jnp.broadcast_to(row, (lanes, order)).T
    upper = jnp.concatenate([column[:half]] * (order // lanes), 1)
    lower = jnp.concatenate([column[half:]] * (half // lanes), 1)
    below = jnp.concatenate(
        [jnp.sum(left * lower, 0, keepdims=True), jnp.sum(low * lower, 0, keepdims=True)], 1
    )
    shift = (jnp.sum(top * upper, 0, keepdims=True) + below) * inv_norm
    gain = jnp.sqrt(order - 1.0) * jnp.sqrt(inv_norm)
    first, rest = slice(0, half), slice(half, None)
    put_at(w_ref, first, slice(None), gain * top + shift)
    put_at(w_ref, rest, rest, gain * low + shift[:, half:])
    put_at(w_ref, rest, first, gain * left + shift[:, :half])


def solve(orders, own_parts, far_parts, own_info, far_info):
    order = sum(part.shape[0] for part in own_parts)
    nobs = own_parts[0].shape[1]
    half = order // 2
    vmem = pl.BlockSpec(memory_space=pltpu.VMEM)
    pair = pltpu.VMEM((2, order, order), BF16)
    nparts = len(own_parts)
    shapes = [(half, order), (half, half), (8, order)]
    own = pl.pallas_call(
        functools.partial(gram_kernel, orders, nparts),
        out_shape=[jax.ShapeDtypeStruct(shape, F32) for shape in shapes],
        in_specs=[vmem] * (nparts + 1),
        out_specs=[vmem] * 3,
        scratch_shapes=[pltpu.VMEM((2, order, nobs), BF16)],
        compiler_params=pltpu.CompilerParams(vmem_limit_bytes=24 << 20),
        cost_estimate=pl.CostEstimate(
            flops=3 * 2 * order**3, bytes_accessed=4 * order * nobs, transcendentals=0
        ),
    )(*own_parts, own_info)
    return pl.pallas_call(
        functools.partial(solve_kernel, orders, nparts),
        out_shape=jax.ShapeDtypeStruct((2, order, order), BF16),
        in_specs=[vmem] * (nparts + 4),
        out_specs=vmem,
        scratch_shapes=[pltpu.VMEM((2, order, nobs), BF16), pair, pair, pair],
        compiler_params=pltpu.CompilerParams(vmem_limit_bytes=40 << 20),
        cost_estimate=pl.CostEstimate(
            flops=21 * 3 * 2 * order**3, bytes_accessed=4 * order * nobs, transcendentals=0
        ),
    )(*far_parts, far_info, *own)


def update_kernel(w_ref, x_ref, o_ref):
    x = x_ref[...]
    center = jnp.mean(x, axis=0, keepdims=True)
    o_ref[...] = center + dot3(get(w_ref), split(x - center))


def update(weights, members):
    vmem = pl.BlockSpec(memory_space=pltpu.VMEM)
    order, cells = members.shape
    return pl.pallas_call(
        update_kernel,
        out_shape=jax.ShapeDtypeStruct(members.shape, F32),
        in_specs=[vmem, vmem],
        out_specs=vmem,
        compiler_params=pltpu.CompilerParams(vmem_limit_bytes=24 << 20),
        cost_estimate=pl.CostEstimate(
            flops=3 * 2 * order * order * cells, bytes_accessed=12 * order * cells, transcendentals=0
        ),
    )(weights, members)


def swap_by(block, count, first, second):
    route = [(i, i ^ first) for i in range(count)]
    route += [(count + i, count + (i ^ second)) for i in range(count)]
    return lax.ppermute(block, ("region", "member"), route)


REGIONS = [(0, 1), (1, 0)]


def from_region(block):
    return lax.ppermute(block, "region", REGIONS)


def gather_rows(shard, facts, blocks, count):
    low = 1 << (count.bit_length() - 1) // 2
    if low != 4 or low * low != count or shard.shape[0] % 16:
        whole = lax.all_gather(shard, "member", axis=0, tiled=True)
        same = list(range(whole.shape[0] // 32))
        info = pack(*facts)
        return (same, same), [whole], [from_region(whole)], info, from_region(info), blocks
    far_steps = [(step * low, step * low) for step in (2, 1, 3)]
    near_steps = [(2, 1), (1, 2), (3, 3)]
    got = [swap_by(shard, count, a, b) for a, b in far_steps]
    held = jnp.concatenate([shard] + got)
    held, facts, blocks = lax.optimization_barrier((held, facts, blocks))
    info, blocks = lax.optimization_barrier((pack(*facts), blocks))
    own = [held] + [swap_by(held, count, a, b) for a, b in near_steps]
    far = [from_region(part) for part in own]
    orders = [
        [n ^ f for n in [0] + [pair[r] for pair in near_steps] for f in [0] + [pair[r] for pair in far_steps]]
        for r in (0, 1)
    ]
    return orders, own, far, info, from_region(info), blocks


def local(state, obs_pert, owners, loc_index, innov, obs_var, loc_scales):
    npatch = lax.axis_size("member")
    facts = (owners, loc_index, innov, obs_var, loc_scales)
    rows, width = state.shape
    blocks = jnp.swapaxes(state.reshape(rows, npatch, width // npatch), 0, 1)
    orders, own, far, info, far_info, blocks = gather_rows(obs_pert[0], facts, blocks, npatch)
    weights = solve(orders, own, far, info, far_info)
    members = lax.all_to_all(blocks, "member", split_axis=0, concat_axis=0, tiled=True)
    updated = update(weights, members.reshape(rows * npatch, width // npatch))
    return lax.all_to_all(updated, "member", split_axis=0, concat_axis=1, tiled=True)


def solution(mesh):
    placed = (
        P("member", "region"),
        P("region", "member", None),
        P("region", None),
        P("region", None),
        P("region", None),
        P("region", None),
        P(),
    )
    return jax.shard_map(
        local, mesh=mesh, in_specs=placed, out_specs=P("member", "region"), check_vma=False
    )
```
